512 devices in a mesh: prow: 8 (over y), pcol: 64 (over z, x, core).
Axes of the slice: x: 4, y: 8, z: 8, core: 2. Of those that a mesh axis runs over, the one named last changes fastest.
Arguments:
- y_root: float32 [16384, 384], P(('prow', 'pcol')), may hold values from -6 to 6
- root_inverse: float32 [16384, 16384], P('prow', 'pcol'), may hold values from -0.046875 to 0.046875
- coupling: float32 [2, 8192, 8192], P(None, 'pcol', 'prow'), may hold values from -0.0625 to 0.0625
- row_list: int32 [2, 8192], P(None, 'pcol'), may hold values from 0 to 16383, as said below
- y_kids: float32 [2, 8192, 384], P(None, 'prow', 'pcol'), may hold values from -6 to 6
- kid_inverse: float32 [2, 8192, 8192], P(None, 'prow', 'pcol'), may hold values from -0.0625 to 0.0625
Outputs:
- x_root: float32 [16384, 384], P('pcol', 'prow')
- x_kids: float32 [2, 8192, 384], P(None, 'pcol', 'prow')
The draws below stay inside these ranges and needn't reach their ends.
Inputs may be any that keep to these rules, and one draw needn't show every extreme that they name: `row_list`: split each child's list into blocks of 8192 / 64 consecutive entries; block j names distinct root rows from j * 256 to (j + 1) * 256 - 1, always including the first and the last of them.
All inputs are finite; a program needn't handle non-finite values.
Results may differ from the reference program's by a relative error of at most 0.0001.
Values sent between devices are 32-bit elements; how exact they have to be, the bound alone decides.
No kernel may reach another device: no remote copies, remote signals or barrier semaphores. Data moves between devices by JAX's collectives and lax.ppermute only.
A program may use at most 64 MiB of HBM per device.

```python
import jax
import jax.numpy as jnp
from jax import lax

N0 = 16384
N1 = 8192
KIDS = 2
SAMPLES = 384
COUPLED = 8192
ROOT_SPAN = 256
N_PCOL = 64


def draw_row_list(key, part):
    span = ROOT_SPAN
    per = COUPLED // N_PCOL
    keys = jax.random.split(key, KIDS * N_PCOL)

    def one_block(block_key):
        inner = jax.random.permutation(block_key, span - 2)[:per - 2] + 1
        ends = jnp.array([0, span - 1], dtype=jnp.int32)
        return jnp.concatenate([ends, inner.astype(jnp.int32)])
    blocks = jax.vmap(one_block)(keys).reshape(KIDS, N_PCOL, per)
    offsets = (jnp.arange(N_PCOL, dtype=jnp.int32) * span)[None, :, None]
    return (blocks + offsets).reshape(KIDS, N_PCOL * per).astype(jnp.int32)


def level_of(rng, shape, cuts, low, top_value):
    def one(axis_at, parts):
        heights = jax.random.uniform(jax.random.fold_in(jax.random.fold_in(rng, 6), axis_at), (parts,), jnp.float32, low / len(cuts), top_value / len(cuts))
        return jnp.repeat(jnp.exp(heights), shape[axis_at] // parts).reshape((-1,) + (1,) * (len(shape) - axis_at - 1))

    gain = one(*cuts[0])
    for cut in cuts[1:]:
        gain = gain * one(*cut)
    return gain


def bell_draw(own_key, extent, deviation, limit, cuts=(), held_as=jnp.bfloat16):
    gain = level_of(own_key, extent, cuts, -0.22, 0.18) if cuts else 1.0
    drawn = jax.random.normal(own_key, extent, jnp.float32) * deviation * gain
    return jnp.minimum(jnp.maximum(drawn, -limit), limit).astype(held_as)


def setup_inputs(seed: int = 0) -> dict:
    splits = jax.random.split(jax.random.key(seed), 7)
    y_root = bell_draw(splits[0], (N0, SAMPLES), 1.0, 6.0, ((0, 512),), jnp.float32)
    root_inverse = bell_draw(splits[1], (N0, N0), N0 ** -0.5, 0.046875, ((0, 8), (1, 64)), jnp.float32)
    coupling = bell_draw(splits[2], (KIDS, COUPLED, N1), COUPLED ** -0.5, 0.0625, ((1, 64), (2, 8)), jnp.float32)
    row_list = draw_row_list(jax.random.fold_in(splits[6], 71), 0)
    y_kids = bell_draw(splits[4], (KIDS, N1, SAMPLES), 1.0, 6.0, ((1, 8), (2, 64)), jnp.float32)
    kid_inverse = bell_draw(splits[5], (KIDS, N1, N1), N1 ** -0.5, 0.0625, ((1, 8), (2, 64)), jnp.float32)
    return dict(y_root=y_root, root_inverse=root_inverse, coupling=coupling, row_list=row_list, y_kids=y_kids, kid_inverse=kid_inverse)


def reference(y_root, root_inverse, coupling, row_list, y_kids, kid_inverse):
    high = lax.Precision.HIGHEST
    x_root = lax.dot_general(root_inverse, y_root, (((0,), (0,)), ((), ())), precision=high, preferred_element_type=jnp.float32)
    outputs = []
    for child in range(KIDS):
        picked = x_root[row_list[child].astype(jnp.int32)]
        update = lax.dot_general(coupling[child], picked, (((0,), (0,)), ((), ())), precision=high, preferred_element_type=jnp.float32)
        reduced = y_kids[child] - update
        solved = lax.dot_general(kid_inverse[child], reduced, (((0,), (0,)), ((), ())), precision=high, preferred_element_type=jnp.float32)
        outputs.append(solved)
    return x_root, jnp.stack(outputs)
```

```python
import jax
import jax.numpy as jnp
from jax import lax
from jax.sharding import PartitionSpec as P

AXES = ("prow", "pcol")
NY, NZ, NX, NC = 8, 8, 4, 2
HIGH = lax.Precision.HIGHEST


def device(y, z, x, c):
    return ((y * NZ + z) * NX + x) * NC + c


def far_groups():
    return [
        [device(y, 2 * zh + pz, 2 * xh + px, c) for zh in range(NZ // 2) for xh in range(NX // 2)]
        for y in range(NY) for pz in range(2) for px in range(2) for c in range(NC)
    ]


def near_groups():
    groups = []
    for y in range(NY):
        for c in range(NC):
            for a in range(NZ // 2):
                for b in range(NX // 2):
                    zs = sorted(((2 * a + c) % NZ, (2 * a + c + 1) % NZ), key=lambda v: v % 2)
                    xs = sorted(((2 * b + c) % NX, (2 * b + c + 1) % NX), key=lambda v: v % 2)
                    groups.append([device(y, z, x, c) for z in zs for x in xs])
    return groups


def row_groups():
    return [
        [device(y, z, x, c) for y in range(NY)]
        for z in range(NZ) for x in range(NX) for c in range(NC)
    ]


FAR, NEAR, ROW = far_groups(), near_groups(), row_groups()


def exchange(parts, groups):
    return lax.all_to_all(parts, AXES, 0, 0, axis_index_groups=groups)


def gather(part, groups):
    return exchange(jnp.broadcast_to(part[None], (len(groups[0]),) + part.shape), groups)


def scatter_sum(parts, groups):
    return jnp.sum(exchange(parts, groups), axis=0)


def swap(value):
    return lax.ppermute(value, AXES, [(i, i ^ 1) for i in range(NY * NZ * NX * NC)])


def dot(a, b):
    return lax.dot_general(
        a, b, (((0,), (0,)), ((), ())), precision=HIGH, preferred_element_type=jnp.float32
    )


def body(y_root, root_inverse, coupling, row_list, y_kids, kid_inverse):
    rows, samples = y_root.shape
    span = root_inverse.shape[1]
    pcol = lax.axis_index("pcol")
    core = pcol % NC
    own = lax.dynamic_index_in_dim

    held = gather(gather(y_root, FAR), NEAR)
    held = held.reshape(2, 2, NZ // 2, NX // 2, rows, samples).transpose(2, 0, 3, 1, 4, 5)
    held = held.reshape(NZ * NX * rows, samples)
    other = swap(held)
    factor = root_inverse.reshape(NZ * NX, NC, rows, span)
    partial_root = dot(held, own(factor, core, 1, False).reshape(NZ * NX * rows, span))
    partial_root += dot(other, own(factor, 1 - core, 1, False).reshape(NZ * NX * rows, span))
    x_root = scatter_sum(partial_root.reshape(NY, samples // NY, span), ROW)
    root_rows = gather(x_root, ROW).reshape(samples, span).T

    local_rows = row_list - pcol * span
    width = y_kids.shape[2]

    def reduced_part(child):
        picked = root_rows[own(local_rows, child, 0, False)]
        update = dot(own(coupling, child, 0, False), picked)
        placed = lax.dynamic_update_slice(
            jnp.zeros_like(update), own(y_kids, child, 0, False), (0, pcol * width)
        )
        return placed - update

    sent = swap(reduced_part(1 - core))
    part = reduced_part(core) + sent
    part = scatter_sum(part.reshape(4, part.shape[0] // 4, samples), NEAR)
    part = scatter_sum(part.reshape(8, part.shape[0] // 8, samples), FAR)
    reduced = gather(gather(part, FAR), NEAR).reshape(-1, samples)
    other = swap(reduced)
    mine = dot(reduced, own(kid_inverse, core, 0, False))
    theirs = dot(other, own(kid_inverse, 1 - core, 0, False))
    kid_part = jnp.where(core == 0, jnp.stack([mine, theirs]), jnp.stack([theirs, mine]))
    kid_part = kid_part.reshape(2, NY, samples // NY, -1).transpose(1, 0, 2, 3)
    x_kids = scatter_sum(kid_part, ROW)
    return x_root.T, x_kids.transpose(0, 2, 1)


def solution(mesh):
    in_specs = (
        P(("prow", "pcol"), None),
        P("prow", "pcol"),
        P(None, "pcol", "prow"),
        P(None, "pcol"),
        P(None, "prow", "pcol"),
        P(None, "prow", "pcol"),
    )
    out_specs = (P("pcol", "prow"), P(None, "pcol", "prow"))
    return jax.shard_map(body, mesh=mesh, in_specs=in_specs, out_specs=out_specs, check_vma=False)
```

```python
import jax
import jax.numpy as jnp
from jax import lax
from jax.sharding import PartitionSpec as P

AXES = ("prow", "pcol")
NY, NZ, NX, NC = 8, 8, 4, 2
PRECISION = lax.Precision.HIGH
pick = lax.dynamic_index_in_dim


def device(y, z, x, c):
    return ((y * NZ + z) * NX + x) * NC + c


def far_groups():
    return [
        [device(y, 2 * zh + pz, 2 * xh + px, c) for zh in range(NZ // 2) for xh in range(NX // 2)]
        for y in range(NY) for pz in range(2) for px in range(2) for c in range(NC)
    ]


def near_groups():
    groups = []
    for y in range(NY):
        for c in range(NC):
            for a in range(NZ // 2):
                for b in range(NX // 2):
                    zs = sorted(((2 * a + c) % NZ, (2 * a + c + 1) % NZ), key=lambda v: v % 2)
                    xs = sorted(((2 * b + c) % NX, (2 * b + c + 1) % NX), key=lambda v: v % 2)
                    groups.append([device(y, z, x, c) for z in zs for x in xs])
    return groups


def row_groups():
    return [
        [device(y, z, x, c) for y in range(NY)]
        for z in range(NZ) for x in range(NX) for c in range(NC)
    ]


def pair_row_groups():
    return [
        [device(y, z, x, c) for y in range(NY) for c in range(NC)]
        for z in range(NZ) for x in range(NX)
    ]


FAR, NEAR, ROW, PAIR_ROW = far_groups(), near_groups(), row_groups(), pair_row_groups()


def exchange(parts, groups):
    return lax.all_to_all(parts, AXES, 0, 0, axis_index_groups=groups)


def gather(part, groups):
    return exchange(jnp.broadcast_to(part[None], (len(groups[0]),) + part.shape), groups)


def scatter_sum(parts, groups):
    return jnp.sum(exchange(parts, groups), axis=0)


def swap(value):
    return lax.ppermute(value, AXES, [(i, i ^ 1) for i in range(NY * NZ * NX * NC)])


def dot(a, b):
    return lax.dot_general(
        a, b, (((0,), (0,)), ((), ())), precision=PRECISION, preferred_element_type=jnp.float32
    )


def body(y_root, root_inverse, coupling, row_list, y_kids, kid_inverse):
    rows, samples = y_root.shape
    span = root_inverse.shape[1]
    width = y_kids.shape[2]
    per = coupling.shape[1]
    prow, pcol = lax.axis_index("prow"), lax.axis_index("pcol")
    core = pcol % NC
    columns = NZ * NX * rows

    factor = root_inverse.reshape(NZ * NX, NC, rows, span)
    near_rows = pick(factor, core, 1, False).reshape(columns, span)
    far_rows = pick(factor, 1 - core, 1, False).reshape(columns, span)
    extended = jnp.concatenate(
        [coupling, y_kids.transpose(0, 2, 1), jnp.zeros((2, 8 - width, coupling.shape[2]))], axis=1
    )
    link, link_other = pick(extended, core, 0, False), swap(pick(extended, 1 - core, 0, False))
    lane = lax.broadcasted_iota(jnp.int32, (8, samples), 1)
    row = lax.broadcasted_iota(jnp.int32, (8, samples), 0)
    spots = [(lane == row + width * q).astype(jnp.float32) for q in (pcol, pcol ^ 1)]
    ahead = dot(jnp.concatenate([link[per:], link_other[per:]]), jnp.concatenate(spots))
    kept, sent = pick(kid_inverse, core, 0, False), swap(pick(kid_inverse, 1 - core, 0, False))
    solve = jnp.concatenate(
        [jnp.where(core == 0, kept, sent), jnp.where(core == 0, sent, kept)], axis=1
    )

    held = gather(y_root, FAR)
    held, near_rows, far_rows = lax.optimization_barrier((held, near_rows, far_rows))
    held = gather(held, NEAR)
    held = held.reshape(2, 2, NZ // 2, NX // 2, rows, samples).transpose(2, 0, 3, 1, 4, 5)
    held = held.reshape(columns, samples)
    partial_root = dot(near_rows, held) + dot(far_rows, swap(held))
    x_part = scatter_sum(partial_root.reshape(NY, span // NY, samples), ROW)
    root_rows = gather(x_part, ROW).reshape(span, samples)
    x_root = lax.dynamic_slice_in_dim(root_rows, prow * (samples // NY), samples // NY, 1)

    local_rows = row_list - pcol * span
    other = swap(root_rows[pick(local_rows, 1 - core, 0, False)])
    total = ahead - dot(link[:per], root_rows[pick(local_rows, core, 0, False)])
    total = total - dot(link_other[:per], other)
    total = scatter_sum(total.reshape(4, columns // 4, samples), NEAR)
    total = scatter_sum(total.reshape(8, rows, samples), FAR)
    reduced = gather(gather(total, FAR), NEAR).reshape(columns, samples)
    solved = lax.optimization_barrier(dot(solve, reduced))
    solved = solved.reshape(NC, -1, NY, samples // NY).transpose(2, 0, 3, 1)
    solved = solved.reshape((NY * NC,) + solved.shape[2:])
    x_kids = exchange(solved, PAIR_ROW).reshape((NY, NC) + solved.shape[1:])
    x_kids = jnp.sum(x_kids, axis=0)
    return x_root, x_kids.transpose(0, 2, 1)


def solution(mesh):
    in_specs = (
        P(("prow", "pcol"), None),
        P("prow", "pcol"),
        P(None, "pcol", "prow"),
        P(None, "pcol"),
        P(None, "prow", "pcol"),
        P(None, "prow", "pcol"),
    )
    out_specs = (P("pcol", "prow"), P(None, "pcol", "prow"))
    return jax.shard_map(body, mesh=mesh, in_specs=in_specs, out_specs=out_specs, check_vma=False)
```

```python
import jax
import jax.numpy as jnp
from jax import lax
from jax.sharding import PartitionSpec as P

AXES = ("prow", "pcol")
NY, NZ, NX, NC = 8, 8, 4, 2
PRECISION = lax.Precision.HIGH
pick = lax.dynamic_index_in_dim


def device(y, z, x, c):
    return ((y * NZ + z) * NX + x) * NC + c


def far_groups():
    return [
        [device(y, 2 * zh + pz, 2 * xh + px, c) for zh in range(NZ // 2) for xh in range(NX // 2)]
        for y in range(NY) for pz in range(2) for px in range(2) for c in range(NC)
    ]


def near_groups():
    groups = []
    for y in range(NY):
        for c in range(NC):
            for a in range(NZ // 2):
                for b in range(NX // 2):
                    zs = sorted(((2 * a + c) % NZ, (2 * a + c + 1) % NZ), key=lambda v: v % 2)
                    xs = sorted(((2 * b + c) % NX, (2 * b + c + 1) % NX), key=lambda v: v % 2)
                    groups.append([device(y, z, x, c) for z in zs for x in xs])
    return groups


def row_groups():
    return [
        [device(y, z, x, c) for y in range(NY)]
        for z in range(NZ) for x in range(NX) for c in range(NC)
    ]


def pair_row_groups():
    return [
        [device(y, z, x, c) for y in range(NY) for c in range(NC)]
        for z in range(NZ) for x in range(NX)
    ]


FAR, NEAR, ROW, PAIR_ROW = far_groups(), near_groups(), row_groups(), pair_row_groups()


def exchange(parts, groups):
    return lax.all_to_all(parts, AXES, 0, 0, axis_index_groups=groups)


def gather(part, groups):
    return exchange(jnp.broadcast_to(part[None], (len(groups[0]),) + part.shape), groups)


def scatter_sum(parts, groups):
    return jnp.sum(exchange(parts, groups), axis=0)


def swap(value):
    return lax.ppermute(value, AXES, [(i, i ^ 1) for i in range(NY * NZ * NX * NC)])


def dot(a, b):
    return lax.dot_general(
        a, b, (((0,), (0,)), ((), ())), precision=PRECISION, preferred_element_type=jnp.float32
    )


def body(y_root, root_inverse, coupling, row_list, y_kids, kid_inverse):
    rows, samples = y_root.shape
    span = root_inverse.shape[1]
    width = y_kids.shape[2]
    per = coupling.shape[1]
    prow, pcol = lax.axis_index("prow"), lax.axis_index("pcol")
    core = pcol % NC
    columns = NZ * NX * rows

    factor = root_inverse.reshape(NZ * NX, NC, rows, span)
    near_rows = pick(factor, core, 1, False).reshape(columns, span)
    far_rows = pick(factor, 1 - core, 1, False).reshape(columns, span)
    extended = jnp.concatenate(
        [coupling, y_kids.transpose(0, 2, 1), jnp.zeros((2, 8 - width, coupling.shape[2]))], axis=1
    )
    link, link_other = pick(extended, core, 0, False), swap(pick(extended, 1 - core, 0, False))
    kept, sent = pick(kid_inverse, core, 0, False), swap(pick(kid_inverse, 1 - core, 0, False))

    held = gather(y_root, FAR)
    solve = jnp.concatenate(
        [jnp.where(core == 0, kept, sent), jnp.where(core == 0, sent, kept)], axis=1
    )
    held, link_other, solve = lax.optimization_barrier((held, link_other, solve))
    lane = lax.broadcasted_iota(jnp.int32, (8, samples), 1)
    row = lax.broadcasted_iota(jnp.int32, (8, samples), 0)
    spots = [(lane == row + width * q).astype(jnp.float32) for q in (pcol, pcol ^ 1)]
    ahead = dot(jnp.concatenate([link[per:], link_other[per:]]), jnp.concatenate(spots))
    held = gather(held, NEAR)
    held = held.reshape(2, 2, NZ // 2, NX // 2, rows, samples).transpose(2, 0, 3, 1, 4, 5)
    held = held.reshape(columns, samples)
    partial_root = dot(near_rows, held) + dot(far_rows, swap(held))
    x_part = scatter_sum(partial_root.reshape(NY, span // NY, samples), ROW)
    root_rows = gather(x_part, ROW).reshape(span, samples)
    x_root = lax.dynamic_slice_in_dim(root_rows, prow * (samples // NY), samples // NY, 1)

    local_rows = row_list - pcol * span
    other = swap(root_rows[pick(local_rows, 1 - core, 0, False)])
    total = ahead - dot(link[:per], root_rows[pick(local_rows, core, 0, False)])
    total = total - dot(link_other[:per], other)
    total = scatter_sum(total.reshape(4, columns // 4, samples), NEAR)
    total = scatter_sum(total.reshape(8, rows, samples), FAR)
    reduced = gather(gather(total, FAR), NEAR).reshape(columns, samples)
    solved = lax.optimization_barrier(dot(solve, reduced))
    solved = solved.reshape(NC, -1, NY, samples // NY).transpose(2, 0, 3, 1)
    solved = solved.reshape((NY * NC,) + solved.shape[2:])
    x_kids = exchange(solved, PAIR_ROW).reshape((NY, NC) + solved.shape[1:])
    x_kids = jnp.sum(x_kids, axis=0)
    return x_root, x_kids.transpose(0, 2, 1)


def solution(mesh):
    in_specs = (
        P(("prow", "pcol"), None),
        P("prow", "pcol"),
        P(None, "pcol", "prow"),
        P(None, "pcol"),
        P(None, "prow", "pcol"),
        P(None, "prow", "pcol"),
    )
    out_specs = (P("pcol", "prow"), P(None, "pcol", "prow"))
    return jax.shard_map(body, mesh=mesh, in_specs=in_specs, out_specs=out_specs, check_vma=False)
```

```python
import jax
import jax.numpy as jnp
from jax import lax
from jax.sharding import PartitionSpec as P

AXES = ("prow", "pcol")
NY, NZ, NX, NC = 8, 8, 4, 2
PRECISION = lax.Precision.HIGH
pick = lax.dynamic_index_in_dim


def device(y, z, x, c):
    return ((y * NZ + z) * NX + x) * NC + c


def far_groups():
    return [
        [device(y, 2 * zh + pz, 2 * xh + px, c) for zh in range(NZ // 2) for xh in range(NX // 2)]
        for y in range(NY) for pz in range(2) for px in range(2) for c in range(NC)
    ]


def near_groups():
    groups = []
    for y in range(NY):
        for c in range(NC):
            for a in range(NZ // 2):
                for b in range(NX // 2):
                    zs = sorted(((2 * a + c) % NZ, (2 * a + c + 1) % NZ), key=lambda v: v % 2)
                    xs = sorted(((2 * b + c) % NX, (2 * b + c + 1) % NX), key=lambda v: v % 2)
                    groups.append([device(y, z, x, c) for z in zs for x in xs])
    return groups


def row_groups():
    return [
        [device(y, z, x, c) for y in range(NY)]
        for z in range(NZ) for x in range(NX) for c in range(NC)
    ]


def pair_row_groups():
    return [
        [device(y, z, x, c) for y in range(NY) for c in range(NC)]
        for z in range(NZ) for x in range(NX)
    ]


FAR, NEAR, ROW, PAIR_ROW = far_groups(), near_groups(), row_groups(), pair_row_groups()


def exchange(parts, groups):
    return lax.all_to_all(parts, AXES, 0, 0, axis_index_groups=groups)


def gather(part, groups):
    return exchange(jnp.broadcast_to(part[None], (len(groups[0]),) + part.shape), groups)


def scatter_sum(parts, groups):
    return jnp.sum(exchange(parts, groups), axis=0)


def swap(value):
    return lax.ppermute(value, AXES, [(i, i ^ 1) for i in range(NY * NZ * NX * NC)])


def halve(value, bit):
    side = lax.axis_index("prow") // bit % 2
    sent = lax.ppermute(
        pick(value, 1 - side, 1, False), "prow", [(i, i ^ bit) for i in range(NY)]
    )
    return pick(value, side, 1, False) + sent


def dot(a, b):
    return lax.dot_general(
        a, b, (((0,), (0,)), ((), ())), precision=PRECISION, preferred_element_type=jnp.float32
    )


def body(y_root, root_inverse, coupling, row_list, y_kids, kid_inverse):
    rows, samples = y_root.shape
    span = root_inverse.shape[1]
    width = y_kids.shape[2]
    per = coupling.shape[1]
    pcol = lax.axis_index("pcol")
    core = pcol % NC
    columns = NZ * NX * rows

    factor = root_inverse.reshape(NZ * NX, NC, rows, span)
    near_rows = pick(factor, core, 1, False).reshape(columns, span)
    far_rows = pick(factor, 1 - core, 1, False).reshape(columns, span)
    extended = jnp.concatenate(
        [coupling, y_kids.transpose(0, 2, 1), jnp.zeros((2, 8 - width, coupling.shape[2]))], axis=1
    )
    link, link_other = pick(extended, core, 0, False), swap(pick(extended, 1 - core, 0, False))

    held = gather(y_root, FAR)
    held, link_other = lax.optimization_barrier((held, link_other))
    own, other = (v[:per].reshape(NY, 1, per // NY, -1) for v in (link, link_other))
    links = jnp.where(
        core == 0, jnp.concatenate([own, other], axis=1), jnp.concatenate([other, own], axis=1)
    ).reshape(2 * per, -1)
    lane = lax.broadcasted_iota(jnp.int32, (8, samples), 1)
    row = lax.broadcasted_iota(jnp.int32, (8, samples), 0)
    spots = [(lane == row + width * q).astype(jnp.float32) for q in (pcol, pcol ^ 1)]
    ahead = dot(jnp.concatenate([link[per:], link_other[per:]]), jnp.concatenate(spots))
    held = gather(held, NEAR)
    held = held.reshape(2, 2, NZ // 2, NX // 2, rows, samples).transpose(2, 0, 3, 1, 4, 5)
    held = held.reshape(columns, samples)
    partial_root = dot(near_rows, held) + dot(far_rows, swap(held))
    share = per // NY
    spots = (row_list - pcol * span).reshape(2, NY, share).transpose(1, 0, 2)
    picked = partial_root[spots.reshape(-1)].reshape(NY, 2 * share, samples)
    picked, kid_inverse = lax.optimization_barrier((picked, kid_inverse))
    kept, sent = pick(kid_inverse, core, 0, False), swap(pick(kid_inverse, 1 - core, 0, False))
    solve = jnp.concatenate(
        [jnp.where(core == 0, kept, sent), jnp.where(core == 0, sent, kept)], axis=1
    )
    picked, x_root = lax.optimization_barrier((scatter_sum(picked, ROW), partial_root.T))
    picked = jnp.broadcast_to(picked.reshape(1, 2, share, samples), (NY, 2, share, samples))
    picked = exchange(picked.reshape(2 * NY, share, samples), PAIR_ROW).reshape(-1, samples)
    picked, solve = lax.optimization_barrier((picked, solve))
    total = ahead - dot(links, picked)
    total = scatter_sum(total.reshape(4, columns // 4, samples), NEAR)
    total = exchange(total.reshape(8, rows, samples), FAR)
    x_root = halve(x_root.reshape(4, 2, samples // NY, span), 1)
    total, x_root = lax.optimization_barrier((total, x_root))
    total = gather(jnp.sum(total, axis=0), FAR)
    x_root = halve(x_root.reshape(2, 2, samples // NY, span), 2)
    total, x_root = lax.optimization_barrier((total, x_root))
    reduced = gather(total, NEAR).reshape(columns, samples)
    reduced, x_root = lax.optimization_barrier((reduced, halve(x_root[None], 4)[0]))
    solved = lax.optimization_barrier(dot(solve, reduced))
    solved = solved.reshape(NC, -1, NY, samples // NY).transpose(2, 0, 3, 1)
    solved = solved.reshape((NY * NC,) + solved.shape[2:])
    x_kids = exchange(solved, PAIR_ROW).reshape((NY, NC) + solved.shape[1:])
    x_kids = jnp.sum(x_kids, axis=0)
    return x_root.T, x_kids.transpose(0, 2, 1)


def solution(mesh):
    in_specs = (
        P(("prow", "pcol"), None),
        P("prow", "pcol"),
        P(None, "pcol", "prow"),
        P(None, "pcol"),
        P(None, "prow", "pcol"),
        P(None, "prow", "pcol"),
    )
    out_specs = (P("pcol", "prow"), P(None, "pcol", "prow"))
    return jax.shard_map(body, mesh=mesh, in_specs=in_specs, out_specs=out_specs, check_vma=False)
```
